32 devices in a mesh: row: 8 (over z, core), col: 4 (over y, x).
Axes of the slice: x: 2, y: 2, z: 4, core: 2. Of those that a mesh axis runs over, the one named last changes fastest.
Arguments:
- trailing: bfloat16 [6144, 3072], P('row', 'col'), may hold values from -6 to 6
- offdiagonal_panel_rows: bfloat16 [2, 6144, 512], P(None, ('row', 'col')), may hold values from -3 to 3
- pivot_diagonal_blocks: bfloat16 [2, 512, 512], replicated, may hold values from -3 to 14, as said below
- coupling: bfloat16 [512, 512], replicated, may hold values from -0.3314563 to 0.3314563, as said below
- pattern: int32 [2, 48], replicated, may hold values 0 or 1
- block_slot_lookup: int32 [48], replicated, may hold values from 0 to 47, each once
- elimination_sequence: int32 [2], replicated, may hold values from 0 to 1, each once
Outputs:
- updated: bfloat16 [6144, 3072], P('row', 'col')
- factor: bfloat16 [2, 6144, 512], P(None, ('row', 'col'))
The draws below stay inside these ranges and needn't reach their ends.
Inputs may be any that keep to these rules, and one draw needn't show every extreme that they name: `pivot_diagonal_blocks`: each diagonal block is symmetric positive definite. `coupling`: pivot_diagonal_blocks[b] - link link^T is positive definite. `elimination_sequence`: a permutation of the two panel indices.
All inputs are finite; a program needn't handle non-finite values.
Results may differ from the reference program's by a relative error of at most 0.0055.
Values may be sent and summed in bfloat16 or wider, within the bound.
A program may use at most 64 MiB of HBM per device.

```python
import jax
import jax.numpy as jnp

B = 128
SN = 512
NB = 48
NC = 24


def draw_pivot_diagonal_blocks(key, part):
    base_key = jax.random.fold_in(key, 3)
    base = jnp.clip(jax.random.normal(base_key, (2, SN, SN), jnp.float32), -3.0, 3.0)
    gram = jnp.einsum('pik,pjk->pij', base, base) / SN
    matrix = 2.0 * jnp.eye(SN, dtype=jnp.float32)[None] + gram
    return matrix.astype(jnp.bfloat16)


def draw_coupling(key, part):
    entry_key = jax.random.fold_in(key, 5)
    spread = 1.05 * SN ** (-0.5)
    raw = jnp.clip(jax.random.normal(entry_key, (SN, SN), jnp.float32), -3.0, 3.0)
    return (raw * spread).astype(jnp.bfloat16)


def set_ends(array, key, smallest, high):
    longest = array.shape.index(max(array.shape))
    spots = []
    for shift in (0, 1):
        where = [jax.random.randint(jax.random.fold_in(key, axis), (), 0, length) for axis, length in enumerate(array.shape)]
        where[longest] = (where[longest] + shift) % array.shape[longest]
        spots.append(tuple(where))
    return array.at[spots[0]].set(smallest).at[spots[1]].set(high)


def levels(own_key, dims, cuts, low, top_value):
    def one(dim, blocks):
        steps = jax.random.uniform(jax.random.fold_in(jax.random.fold_in(own_key, 6), dim), (blocks,), jnp.float32, low / len(cuts), top_value / len(cuts))
        return jnp.repeat(jnp.exp(steps), dims[dim] // blocks).reshape((-1,) + (1,) * (len(dims) - dim - 1))

    gain = one(*cuts[0])
    for cut in cuts[1:]:
        gain = gain * one(*cut)
    return gain


def centred(rng, shape, width, reach, pieces=(), kind=jnp.bfloat16):
    factor_of = levels(rng, shape, pieces, -0.22, 0.18) if pieces else 1.0
    values = jax.random.normal(rng, shape, jnp.float32) * width * factor_of
    return jnp.minimum(jnp.maximum(values, -reach), reach).astype(kind)


def setup_inputs(seed: int = 0) -> dict:
    seeds = jax.random.split(jax.random.key(seed), 8)
    return {
        "trailing": centred(seeds[0], (NB * B, NC * B), 1.0, 6.0, ((0, 8), (1, 4))),
        "offdiagonal_panel_rows": centred(seeds[1], (2, NB * B, SN), 0.4, 3.0, ((1, 32),)),
        "pivot_diagonal_blocks": draw_pivot_diagonal_blocks(jax.random.fold_in(seeds[7], 71), 0),
        "coupling": draw_coupling(jax.random.fold_in(seeds[7], 71), 0),
        "pattern": set_ends((jax.random.randint(seeds[4], (2, NB), 0, 3) < 2).astype(jnp.int32), jax.random.fold_in(seeds[4], 1), 0, 1),
        "block_slot_lookup": jax.random.permutation(seeds[5], NB).astype(jnp.int32),
        "elimination_sequence": jax.random.permutation(seeds[6], 2).astype(jnp.int32),
    }


def solve_right(rhs, lower_factor):
    return jax.scipy.linalg.solve_triangular(lower_factor, rhs.T, lower=True).T

def reference(trailing, offdiagonal_panel_rows, pivot_diagonal_blocks, coupling, pattern, block_slot_lookup, elimination_sequence):
    total_rows = offdiagonal_panel_rows.shape[1]
    slots = (jnp.arange(total_rows, dtype=jnp.int32) // B).astype(jnp.int32)
    global_block = block_slot_lookup[slots]
    keep_mask = pattern[:, global_block].astype(jnp.float32)
    masked = offdiagonal_panel_rows.astype(jnp.float32) * keep_mask[:, :, None]
    exchanged_panels = elimination_sequence[0] == 1
    sorted_panels = jnp.where(exchanged_panels, masked[::-1], masked)
    diagonals = pivot_diagonal_blocks.astype(jnp.float32)
    diagonals = jnp.where(exchanged_panels, diagonals[::-1], diagonals)
    couple = coupling.astype(jnp.float32)
    kmat = jnp.where(exchanged_panels, couple.T, couple)
    first_factor = jnp.linalg.cholesky(diagonals[0])
    leading_rows = solve_right(sorted_panels[0], first_factor).astype(jnp.bfloat16)
    link = solve_right(kmat, first_factor).astype(jnp.bfloat16)
    shrunk = diagonals[1] - jnp.dot(link.astype(jnp.float32), link.T.astype(jnp.float32), preferred_element_type=jnp.float32)
    second_factor = jnp.linalg.cholesky(shrunk)
    updated_rows = sorted_panels[1] - jnp.dot(leading_rows.astype(jnp.float32), link.T.astype(jnp.float32), preferred_element_type=jnp.float32)
    second_rows = solve_right(updated_rows, second_factor).astype(jnp.bfloat16)
    columns = NC * B
    result = trailing.astype(jnp.float32)
    result = result - jnp.dot(leading_rows.astype(jnp.float32), leading_rows[:columns].T.astype(jnp.float32), preferred_element_type=jnp.float32)
    result = result - jnp.dot(second_rows.astype(jnp.float32), second_rows[:columns].T.astype(jnp.float32), preferred_element_type=jnp.float32)
    stacked = jnp.stack([leading_rows, second_rows])
    factor = jnp.where(exchanged_panels, stacked[::-1], stacked)
    return (result.astype(jnp.bfloat16), factor)
```

```python
import functools

import jax
import jax.numpy as jnp
from jax import lax
from jax.experimental import pallas as pl
from jax.experimental.pallas import tpu as pltpu
from jax.sharding import PartitionSpec as P

B = 128


def from_root(value, axis, source):
    kept = jnp.where(lax.axis_index(axis) == source, value, 0).astype(value.dtype)
    return lax.psum(kept, axis)


def solve_right(rhs, lower_factor):
    return jax.scipy.linalg.solve_triangular(lower_factor, rhs.T, lower=True).T


def product_rows(left, right):
    return lax.dot_general(
        left, right, (((1,), (1,)), ((), ())), preferred_element_type=jnp.float32
    )


def direct(
    trailing,
    offdiagonal_panel_rows,
    pivot_diagonal_blocks,
    coupling,
    pattern,
    block_slot_lookup,
    elimination_sequence,
):
    width = offdiagonal_panel_rows.shape[1]
    col_count = lax.axis_size("col")
    row_index = lax.axis_index("row")
    col_index = lax.axis_index("col")
    first_row = (row_index * col_count + col_index) * width
    slots = (first_row + jnp.arange(width, dtype=jnp.int32)) // B
    total_blocks = block_slot_lookup.shape[0]
    every_block = jnp.arange(total_blocks, dtype=jnp.int32)
    slot_hit = (slots[:, None] == every_block[None, :]).astype(jnp.int32)
    global_block = jnp.sum(slot_hit * block_slot_lookup[None, :], axis=1)
    block_hit = (global_block[:, None] == every_block[None, :]).astype(jnp.int32)
    keep_mask = jnp.sum(pattern[:, None, :] * block_hit[None], axis=2)
    masked = offdiagonal_panel_rows * keep_mask[:, :, None].astype(jnp.bfloat16)
    exchanged_panels = elimination_sequence[0] == 1
    sorted_panels = jnp.where(exchanged_panels, masked[::-1], masked)
    diagonals = pivot_diagonal_blocks.astype(jnp.float32)
    diagonals = jnp.where(exchanged_panels, diagonals[::-1], diagonals)
    couple = coupling.astype(jnp.float32)
    kmat = jnp.where(exchanged_panels, couple.T, couple)
    first_factor = jnp.linalg.cholesky(diagonals[0])
    link = solve_right(kmat, first_factor).astype(jnp.bfloat16)
    shrunk = diagonals[1] - product_rows(link, link)
    second_factor = jnp.linalg.cholesky(shrunk)
    whole_rows = lax.all_gather(sorted_panels, "col", axis=1, tiled=True)
    leading_rows = solve_right(whole_rows[0].astype(jnp.float32), first_factor).astype(jnp.bfloat16)
    updated_rows = whole_rows[1].astype(jnp.float32) - product_rows(leading_rows, link)
    second_rows = solve_right(updated_rows, second_factor).astype(jnp.bfloat16)
    row_factor = jnp.stack([leading_rows, second_rows])
    local_factor = lax.dynamic_slice_in_dim(row_factor, col_index * width, width, 1)
    col_factor = from_root(row_factor, "row", col_index)
    result = trailing.astype(jnp.float32)
    left_operand = jnp.concatenate([row_factor[0], row_factor[1]], axis=1)
    right_side = jnp.concatenate([col_factor[0], col_factor[1]], axis=1)
    result = result - product_rows(left_operand, right_side)
    factor = jnp.where(exchanged_panels, local_factor[::-1], local_factor)
    return (result.astype(jnp.bfloat16), factor)


CORES = 2
MESH = pl.DeviceIdType.MESH
TOLERANCE = 0.01
F32 = jnp.float32
BF16 = jnp.bfloat16


def nt(left, right):
    return lax.dot_general(left, right, (((1,), (1,)), ((), ())), preferred_element_type=F32)


def nn(left, right):
    return lax.dot_general(left, right, (((1,), (0,)), ((), ())), preferred_element_type=F32)


def split(value):
    high = value.astype(BF16)
    return high, (value - high.astype(F32)).astype(BF16)


def tiles(order):
    step = 256 if order % 256 == 0 else order
    return [(start, step) for start in range(0, order, step)]


def places(start, rows, columns):
    row = start + lax.broadcasted_iota(jnp.int32, (rows, columns), 0)
    column = lax.broadcasted_iota(jnp.int32, (rows, columns), 1)
    return row, column


def lower_half(value, start):
    row, column = places(start, *value.shape)
    return jnp.where(column < row, value, jnp.where(column == row, 0.5 * value, 0.0))


def less_identity(value, start):
    row, column = places(start, *value.shape)
    return value - jnp.where(row == column, 1.0, 0.0)


def correct(f_ref, x_ref, order):
    for start, rows in tiles(order):
        part = pl.ds(start, rows)
        f = f_ref[part, :]
        square = nt(f, f_ref[...])
        x_ref[part, :] = (f.astype(F32) - lower_half(square, start)).astype(BF16)


def open_inverse(a_ref, w_ref, f_ref, x_ref):
    order = a_ref.shape[0]
    a = a_ref[...].astype(F32)
    row, column = places(0, order, order)
    on_diagonal = jnp.where(row == column, a, 0.0)
    down = lax.rsqrt(jnp.sum(on_diagonal, axis=1, keepdims=True))
    across = lax.rsqrt(jnp.sum(on_diagonal, axis=0, keepdims=True))
    f_ref[...] = jnp.where(column < row, a * down * across, 0.0).astype(BF16)
    correct(f_ref, x_ref, order)
    for start, rows in tiles(order):
        part = pl.ds(start, rows)
        x = x_ref[part, :]
        square = nn(x, x_ref[...])
        unit = -less_identity(jnp.zeros((rows, order), F32), start)
        w_ref[part, :] = ((unit - x.astype(F32) + square) * across).astype(BF16)


def cubic_inverse(a_ref, w_ref, f_ref, x_ref, y_ref):
    order = a_ref.shape[0]
    for start, rows in tiles(order):
        part = pl.ds(start, rows)
        image = nn(w_ref[part, :], a_ref[...]).astype(BF16)
        error = less_identity(nt(image, w_ref[...]), start)
        f_ref[part, :] = lower_half(error, start).astype(BF16)
    correct(f_ref, x_ref, order)
    for start, rows in tiles(order):
        part = pl.ds(start, rows)
        y_ref[part, :] = nn(x_ref[part, :], w_ref[...])
    later = y_ref[...].astype(BF16)
    for start, rows in tiles(order):
        part = pl.ds(start, rows)
        new = w_ref[part, :].astype(F32) - y_ref[part, :] + nn(x_ref[part, :], later)
        w_ref[part, :] = new.astype(BF16)


def close_inverse(a_ref, rest_ref, w_ref, f_ref, high_ref, low_ref):
    order = a_ref.shape[0]
    total = jnp.zeros((1, order), F32)
    for start, rows in tiles(order):
        part = pl.ds(start, rows)
        image = nn(w_ref[part, :], a_ref[...])
        if rest_ref is not None:
            image = image + nn(w_ref[part, :], rest_ref[...])
        high, low = split(image)
        error = less_identity(nt(high, w_ref[...]) + nt(low, w_ref[...]), start)
        f = lower_half(error, start)
        total = total + jnp.sum(f * f, axis=0, keepdims=True)
        f_ref[part, :] = f.astype(BF16)
    for start, rows in tiles(order):
        part = pl.ds(start, rows)
        new = w_ref[part, :].astype(F32) - nn(f_ref[part, :], w_ref[...])
        high, low = split(new)
        high_ref[part, :] = high
        if low_ref is not None:
            low_ref[part, :] = low
    return total


def kernel(
    col_count, row_count,
    trailing_ref, panels_ref, diagonals_ref, coupling_ref, pattern_ref, lookup_ref, sequence_ref,
    updated_ref, factor_ref, residual_ref,
    row_rows, col_rows, a_ref, rest_ref, k_ref, w_ref, f_ref, x_ref, y_ref,
    first_ref, low_ref, link_ref, second_ref, row_factor, col_factor, held,
    row_send, row_recv, col_send, col_recv, held_sem,
):
    r = lax.axis_index("row")
    c = lax.axis_index("col")
    width, order = panels_ref.shape[1], panels_ref.shape[2]
    z, source_z, last_z = r // CORES, c // CORES, row_count // CORES - 1
    main = r % CORES == c % CORES
    sibling = z * CORES + (CORES - 1 - r % CORES)
    is_source = r == c
    sends = (
        (main & (z >= source_z) & (z < last_z), jnp.minimum(r + CORES, row_count - 1)),
        (main & (z <= source_z) & (z > 0), jnp.maximum(r - CORES, 0)),
        (main, sibling),
    )

    fetch = pltpu.make_async_copy(trailing_ref, held, held_sem)
    fetch.start()

    barrier = pltpu.get_barrier_semaphore()
    for step in range(1, col_count):
        pl.semaphore_signal(barrier, inc=1, device_id=(r, (c + step) % col_count), device_id_type=MESH)
    pl.semaphore_signal(barrier, inc=1, device_id=(sibling, c), device_id_type=MESH)

    @pl.when(z < last_z)
    def _():
        pl.semaphore_signal(barrier, inc=1, device_id=(r + CORES, c), device_id_type=MESH)

    @pl.when(z > 0)
    def _():
        pl.semaphore_signal(barrier, inc=1, device_id=(r - CORES, c), device_id_type=MESH)

    first_row = (r * col_count + c) * width
    first_slot = first_row // B
    slot_count = lookup_ref.shape[0]
    slot_of_row = (first_row + lax.broadcasted_iota(jnp.int32, (width, order), 0)) // B
    for panel in range(2):
        which = sequence_ref[panel]
        kept = jnp.zeros((width, order), jnp.int32)
        for step in range((width + B - 2) // B + 1):
            slot = jnp.minimum(first_slot + step, slot_count - 1)
            flag = pattern_ref[which, lookup_ref[slot]]
            kept = jnp.where(slot_of_row == first_slot + step, flag, kept)
        values = panels_ref[which].astype(F32)
        row_rows[c, panel] = jnp.where(kept == 1, values, 0.0).astype(BF16)

    neighbours = col_count + (z < last_z).astype(jnp.int32) + (z > 0).astype(jnp.int32)
    pl.semaphore_wait(barrier, neighbours)

    def row_copy(step):
        target = (r + step) % col_count
        return target != c, pltpu.make_async_remote_copy(
            src_ref=row_rows.at[c], dst_ref=row_rows.at[c],
            send_sem=row_send.at[step], recv_sem=row_recv.at[c],
            device_id=(r, target), device_id_type=MESH,
        )

    def row_wait(piece):
        pltpu.make_async_remote_copy(
            src_ref=row_rows.at[piece], dst_ref=row_rows.at[piece],
            send_sem=row_send.at[0], recv_sem=row_recv.at[piece],
            device_id=(r, c), device_id_type=MESH,
        ).wait_recv()

    def col_copy(step, panel, way, target):
        piece = (c + step) % col_count
        chunk = 2 * step + panel
        return pltpu.make_async_remote_copy(
            src_ref=col_rows.at[piece, panel], dst_ref=col_rows.at[piece, panel],
            send_sem=col_send.at[way, chunk], recv_sem=col_recv.at[chunk],
            device_id=(target, c), device_id_type=MESH,
        )

    for step in range(col_count):
        wanted, copy = row_copy(step)
        pl.when(wanted)(copy.start)

    def forward(step, panel, arrived=False):
        piece = (c + step) % col_count

        @pl.when(is_source)
        def _():
            if step > 0 and panel == 0 and not arrived:
                row_wait(piece)
            col_rows[piece, panel] = row_rows[piece, panel]

        @pl.when(jnp.logical_not(is_source))
        def _():
            col_copy(step, panel, 0, sibling).wait_recv()

        for way, (wanted, target) in enumerate(sends):
            pl.when(wanted)(col_copy(step, panel, way, target).start)

    chunks = [(step, panel) for step in range(col_count) for panel in range(2)]
    turn = iter(chunks)
    share = -(-len(chunks) // 8)

    def relay():
        for _ in range(share):
            chunk = next(turn, None)
            if chunk is not None:
                forward(*chunk)

    a_ref[...] = diagonals_ref[sequence_ref[0]]
    k = coupling_ref[...].astype(F32)
    k_ref[...] = jnp.where(sequence_ref[0] == 1, k.T, k).astype(BF16)
    open_inverse(a_ref, w_ref, f_ref, x_ref)
    relay()
    cubic_inverse(a_ref, w_ref, f_ref, x_ref, y_ref)
    relay()
    total = close_inverse(a_ref, None, w_ref, f_ref, first_ref, low_ref)
    relay()
    link_ref[...] = (nt(k_ref[...], first_ref[...]) + nt(k_ref[...], low_ref[...])).astype(BF16)
    shrunk = diagonals_ref[sequence_ref[1]].astype(F32) - nt(link_ref[...], link_ref[...])
    high, low = split(shrunk)
    a_ref[...] = high
    rest_ref[...] = low
    open_inverse(a_ref, w_ref, f_ref, x_ref)
    relay()
    cubic_inverse(a_ref, w_ref, f_ref, x_ref, y_ref)
    relay()
    cubic_inverse(a_ref, w_ref, f_ref, x_ref, y_ref)
    relay()
    total = jnp.maximum(total, close_inverse(a_ref, rest_ref, w_ref, f_ref, second_ref, None))
    relay()
    residual_ref[...] = jnp.broadcast_to(jnp.sum(total, axis=1, keepdims=True), residual_ref.shape)

    def factor_rows(rows, factors):
        leading = nt(rows[0], first_ref[...]).astype(BF16)
        factors[:, :order] = leading
        rest = rows[1].astype(F32) - nt(leading, link_ref[...])
        factors[:, order:] = nt(rest.astype(BF16), second_ref[...]).astype(BF16)

    def pieces(ref):
        return [ref[:, panel].reshape(col_count * width, order) for panel in range(2)]

    left = list(turn)
    late = [step for step, panel in left if panel == 0]
    for step in range(1, col_count):
        wait = functools.partial(row_wait, (c + step) % col_count)
        if step in late:
            wait()
        else:
            pl.when(jnp.logical_not(is_source))(wait)
    factor_rows(pieces(row_rows), row_factor)
    own = row_factor[pl.ds(pl.multiple_of(c * width, 16), width), :]
    swapped = sequence_ref[0] == 1
    mine = own[:, :order].astype(F32), own[:, order:].astype(F32)
    factor_ref[0] = jnp.where(swapped, mine[1], mine[0]).astype(BF16)
    factor_ref[1] = jnp.where(swapped, mine[0], mine[1]).astype(BF16)
    for chunk in left:
        forward(*chunk, arrived=True)
    factor_rows(pieces(col_rows), col_factor)

    fetch.wait()
    height = held.shape[0]
    for start in range(0, height, 256):
        part = pl.ds(start, min(256, height - start))
        change = nt(row_factor[part, :], col_factor[...])
        updated_ref[part, :] = (held[part, :].astype(F32) - change).astype(BF16)

    for step in range(col_count):
        wanted, copy = row_copy(step)
        pl.when(wanted)(copy.wait_send)
    for step, panel in chunks:
        for way, (wanted, target) in enumerate(sends):
            pl.when(wanted)(col_copy(step, panel, way, target).wait_send)


def local(col_count, row_count, trailing, panels, diagonals, coupling, pattern, lookup, sequence):
    width, order = panels.shape[1], panels.shape[2]
    rows, columns = trailing.shape
    vmem = pl.BlockSpec(memory_space=pltpu.VMEM)
    smem = pl.BlockSpec(memory_space=pltpu.SMEM)
    square = (order, order)
    rest = (trailing, panels, diagonals, coupling, pattern, lookup, sequence)
    updated, factor, residual = pl.pallas_call(
        functools.partial(kernel, col_count, row_count),
        out_shape=(
            jax.ShapeDtypeStruct(trailing.shape, BF16),
            jax.ShapeDtypeStruct(panels.shape, BF16),
            jax.ShapeDtypeStruct((8, 128), F32),
        ),
        in_specs=[pl.BlockSpec(memory_space=pl.ANY), vmem, vmem, vmem, smem, smem, smem],
        out_specs=(vmem, vmem, vmem),
        scratch_shapes=[
            pltpu.VMEM((col_count, 2, width, order), BF16),
            pltpu.VMEM((col_count, 2, width, order), BF16),
            pltpu.VMEM(square, BF16), pltpu.VMEM(square, BF16), pltpu.VMEM(square, BF16),
            pltpu.VMEM(square, BF16), pltpu.VMEM(square, BF16), pltpu.VMEM(square, BF16),
            pltpu.VMEM(square, F32),
            pltpu.VMEM(square, BF16), pltpu.VMEM(square, BF16), pltpu.VMEM(square, BF16),
            pltpu.VMEM(square, BF16),
            pltpu.VMEM((rows, 2 * order), BF16), pltpu.VMEM((columns, 2 * order), BF16),
            pltpu.VMEM((rows, columns), BF16),
            pltpu.SemaphoreType.DMA((col_count,)), pltpu.SemaphoreType.DMA((col_count,)),
            pltpu.SemaphoreType.DMA((3, 2 * col_count)), pltpu.SemaphoreType.DMA((2 * col_count,)),
            pltpu.SemaphoreType.DMA,
        ],
        compiler_params=pltpu.CompilerParams(
            collective_id=0, has_side_effects=True, vmem_limit_bytes=48 * 2**20
        ),
        cost_estimate=pl.CostEstimate(flops=10**10, bytes_accessed=6 * 10**6, transcendentals=0),
    )(*rest)
    return lax.cond(
        residual[0, 0] < TOLERANCE,
        lambda *_: (updated, factor),
        lambda *args: direct(*args),
        *rest,
    )


def solution(mesh):
    return jax.shard_map(
        functools.partial(local, mesh.shape["col"], mesh.shape["row"]),
        mesh=mesh,
        in_specs=(P("row", "col"), P(None, ("row", "col"), None), P(), P(), P(), P(), P()),
        out_specs=(P("row", "col"), P(None, ("row", "col"), None)),
        check_vma=False,
    )
```

```python
import functools

import jax
import jax.numpy as jnp
from jax import lax
from jax.experimental import pallas as pl
from jax.experimental.pallas import tpu as pltpu
from jax.sharding import PartitionSpec as P

B = 128
CORES = 2
MESH = pl.DeviceIdType.MESH
TOLERANCE = 0.01
F32 = jnp.float32
BF16 = jnp.bfloat16


def nt(left, right):
    return lax.dot_general(left, right, (((1,), (1,)), ((), ())), preferred_element_type=F32)


def nn(left, right):
    return lax.dot_general(left, right, (((1,), (0,)), ((), ())), preferred_element_type=F32)


def split(value):
    high = value.astype(BF16)
    return high, (value - high.astype(F32)).astype(BF16)


def blocks(order):
    size = 256 if order % 256 == 0 else order
    return size, order // size


def place(index, size):
    return pl.ds(index * size, size)


def ramp(index, size):
    return pl.ds(0, (index + 1) * size)


def on_diagonal(size):
    row = lax.broadcasted_iota(jnp.int32, (size, size), 0)
    column = lax.broadcasted_iota(jnp.int32, (size, size), 1)
    return row, column


def lower_half(value, i, j):
    if j < i:
        return value
    row, column = on_diagonal(value.shape[0])
    return jnp.where(column < row, value, jnp.where(column == row, 0.5 * value, 0.0))


def less_identity(value, i, j):
    if j < i:
        return value
    row, column = on_diagonal(value.shape[0])
    return value - jnp.where(row == column, 1.0, 0.0)


def correct(f_ref, x_ref, tick):
    size, count = blocks(f_ref.shape[0])
    for i in range(count):
        for j in range(i + 1):
            square = nt(f_ref[place(i, size), ramp(j, size)], f_ref[place(j, size), ramp(j, size)])
            f = f_ref[place(i, size), place(j, size)].astype(F32)
            x_ref[place(i, size), place(j, size)] = (f - lower_half(square, i, j)).astype(BF16)
        tick()


def lower_product(x_ref, y_ref, i, j, size):
    middle = pl.ds(j * size, (i - j + 1) * size)
    return nn(x_ref[place(i, size), middle], y_ref[middle, place(j, size)])


def open_inverse(a_ref, w_ref, f_ref, x_ref, tick):
    size, count = blocks(a_ref.shape[0])
    row, column = on_diagonal(size)
    across = []
    for i in range(count):
        a = a_ref[place(i, size), place(i, size)].astype(F32)
        diagonal = jnp.where(row == column, a, 0.0)
        down = lax.rsqrt(jnp.sum(diagonal, axis=1, keepdims=True))
        across.append(lax.rsqrt(jnp.sum(diagonal, axis=0, keepdims=True)))
        for j in range(i + 1):
            f = a_ref[place(i, size), place(j, size)].astype(F32) * down * across[j]
            if i == j:
                f = jnp.where(column < row, f, 0.0)
            f_ref[place(i, size), place(j, size)] = f.astype(BF16)
    correct(f_ref, x_ref, tick)
    for i in range(count):
        for j in range(i + 1):
            x = x_ref[place(i, size), place(j, size)].astype(F32)
            new = lower_product(x_ref, x_ref, i, j, size) - x
            if i == j:
                new = new + jnp.where(row == column, 1.0, 0.0)
            w_ref[place(i, size), place(j, size)] = (new * across[j]).astype(BF16)
        tick()


def cubic_inverse(a_ref, w_ref, f_ref, x_ref, y_ref, tick):
    size, count = blocks(a_ref.shape[0])
    for i in range(count):
        own = ramp(i, size)
        image = nn(w_ref[place(i, size), own], a_ref[own, own]).astype(BF16)
        for j in range(i + 1):
            square = nt(image[:, : (j + 1) * size], w_ref[place(j, size), ramp(j, size)])
            f = lower_half(less_identity(square, i, j), i, j)
            f_ref[place(i, size), place(j, size)] = f.astype(BF16)
        tick()
    correct(f_ref, x_ref, tick)
    for i in range(count):
        for j in range(i + 1):
            y_ref[place(i, size), place(j, size)] = lower_product(x_ref, w_ref, i, j, size).astype(BF16)
        tick()
    for i in range(count):
        for j in range(i + 1):
            spot = place(i, size), place(j, size)
            change = lower_product(x_ref, y_ref, i, j, size) - y_ref[spot].astype(F32)
            w_ref[spot] = (w_ref[spot].astype(F32) + change).astype(BF16)
        tick()


def close_inverse(a_ref, rest_ref, w_ref, f_ref, high_ref, low_ref, tick):
    size, count = blocks(a_ref.shape[0])
    total = jnp.zeros((1, size), F32)
    for i in range(count):
        own = ramp(i, size)
        image = nn(w_ref[place(i, size), own], a_ref[own, own])
        if rest_ref is not None:
            image = image + nn(w_ref[place(i, size), own], rest_ref[own, own])
        high, low = split(image)
        for j in range(i + 1):
            far = (j + 1) * size
            beside = w_ref[place(j, size), ramp(j, size)]
            square = nt(high[:, :far], beside) + nt(low[:, :far], beside)
            f = lower_half(less_identity(square, i, j), i, j)
            total = total + jnp.sum(f * f, axis=0, keepdims=True)
            f_ref[place(i, size), place(j, size)] = f.astype(BF16)
        tick()
    for i in range(count):
        for j in range(i + 1):
            spot = place(i, size), place(j, size)
            new = w_ref[spot].astype(F32) - lower_product(f_ref, w_ref, i, j, size)
            high_ref[spot], low_ref[spot] = split(new)
        tick()
    return total


def solved(high, high_ref, low_ref, low=None):
    size, count = blocks(high_ref.shape[0])
    parts = []
    for j in range(count):
        far = (j + 1) * size
        beside = high_ref[place(j, size), ramp(j, size)]
        part = nt(high[:, :far], beside) + nt(high[:, :far], low_ref[place(j, size), ramp(j, size)])
        if low is not None:
            part = part + nt(low[:, :far], beside)
        parts.append(part)
    return jnp.concatenate(parts, axis=1) if count > 1 else parts[0]


def lead(rows, factors, first_ref, low_ref):
    order = first_ref.shape[0]
    factors[:, :order] = solved(rows[0], first_ref, low_ref).astype(BF16)


def follow(rows, factors, link_ref, second_ref, rest_ref):
    order = link_ref.shape[0]
    rest = rows[1].astype(F32) - nt(factors[:, :order], link_ref[...])
    high, low = split(rest)
    factors[:, order:] = solved(high, second_ref, rest_ref, low).astype(BF16)


def pieces(ref):
    count, _, width, order = ref.shape
    return [ref[:, panel].reshape(count * width, order) for panel in range(2)]


def write_factor(row_factor, factor_ref, sequence_ref, c):
    width, order = factor_ref.shape[1], factor_ref.shape[2]
    own = row_factor[pl.ds(pl.multiple_of(c * width, 16), width), :]
    swapped = sequence_ref[0] == 1
    mine = own[:, :order].astype(F32), own[:, order:].astype(F32)
    factor_ref[0] = jnp.where(swapped, mine[1], mine[0]).astype(BF16)
    factor_ref[1] = jnp.where(swapped, mine[0], mine[1]).astype(BF16)


def write_updated(row_factor, col_factor, held, updated_ref):
    height = held.shape[0]
    for start in range(0, height, 256):
        part = pl.ds(start, min(256, height - start))
        change = nt(row_factor[part, :], col_factor[...])
        updated_ref[part, :] = (held[part, :].astype(F32) - change).astype(BF16)


def eliminate(a_ref, w_ref, high_ref, low_ref):
    order = a_ref.shape[0]
    row = lax.broadcasted_iota(jnp.int32, (order, order), 0)
    column = lax.broadcasted_iota(jnp.int32, (order, order), 1)
    w_ref[...] = jnp.where(row == column, 1.0, 0.0)

    def step(j, carry):
        pivot_row = a_ref[pl.ds(j, 1), :]
        lane = lax.broadcasted_iota(jnp.int32, (1, order), 1)
        pivot = jnp.sum(jnp.where(lane == j, pivot_row, 0.0), axis=1, keepdims=True)
        scale = lax.rsqrt(pivot)
        pivot_row = pivot_row * scale
        done = w_ref[pl.ds(j, 1), :] * scale
        a = a_ref[...]
        below = jnp.sum(jnp.where(column == j, a, 0.0), axis=1, keepdims=True) * scale
        below = jnp.where(row[:, :1] > j, below, 0.0)
        a_ref[...] = a - below * pivot_row
        w_ref[...] = w_ref[...] - below * done
        w_ref[pl.ds(j, 1), :] = done
        return carry

    lax.fori_loop(0, order, step, 0)
    high_ref[...], low_ref[...] = split(w_ref[...])


def slow_kernel(
    trailing_ref, row_rows, col_rows, diagonals_ref, coupling_ref, sequence_ref,
    updated_ref, factor_ref,
    a_ref, w_ref, k_ref, first_ref, low_ref, link_ref, second_ref, rest_ref, row_factor, col_factor,
):
    a_ref[...] = diagonals_ref[sequence_ref[0]].astype(F32)
    k = coupling_ref[...].astype(F32)
    k_ref[...] = jnp.where(sequence_ref[0] == 1, k.T, k).astype(BF16)
    eliminate(a_ref, w_ref, first_ref, low_ref)
    link_ref[...] = solved(k_ref[...], first_ref, low_ref).astype(BF16)
    a_ref[...] = diagonals_ref[sequence_ref[1]].astype(F32) - nt(link_ref[...], link_ref[...])
    eliminate(a_ref, w_ref, second_ref, rest_ref)
    for rows, factors in ((row_rows, row_factor), (col_rows, col_factor)):
        lead(pieces(rows), factors, first_ref, low_ref)
        follow(pieces(rows), factors, link_ref, second_ref, rest_ref)
    write_factor(row_factor, factor_ref, sequence_ref, lax.axis_index("col"))
    write_updated(row_factor, col_factor, trailing_ref, updated_ref)


def kernel(
    col_count, row_count,
    trailing_ref, panels_ref, diagonals_ref, coupling_ref, pattern_ref, lookup_ref, sequence_ref,
    updated_ref, factor_ref, residual_ref, row_out, col_out,
    row_rows, col_rows, a_ref, rest_ref, k_ref, w_ref, f_ref, x_ref, y_ref,
    first_ref, low_ref, link_ref, second_ref, last_ref, row_factor, col_factor, held,
    row_send, row_recv, col_send, col_recv, held_sem, out_sem,
):
    r = lax.axis_index("row")
    c = lax.axis_index("col")
    width, order = panels_ref.shape[1], panels_ref.shape[2]
    z, source_z, last_z = r // CORES, c // CORES, row_count // CORES - 1
    main = r % CORES == c % CORES
    sibling = z * CORES + (CORES - 1 - r % CORES)
    is_source = r == c
    sends = (
        (main & (z >= source_z) & (z < last_z), jnp.minimum(r + CORES, row_count - 1)),
        (main & (z <= source_z) & (z > 0), jnp.maximum(r - CORES, 0)),
        (main, sibling),
    )

    fetch = pltpu.make_async_copy(trailing_ref, held, held_sem)
    fetch.start()

    barrier = pltpu.get_barrier_semaphore()
    for step in range(1, col_count):
        pl.semaphore_signal(barrier, inc=1, device_id=(r, (c + step) % col_count), device_id_type=MESH)
    pl.semaphore_signal(barrier, inc=1, device_id=(sibling, c), device_id_type=MESH)

    @pl.when(z < last_z)
    def _():
        pl.semaphore_signal(barrier, inc=1, device_id=(r + CORES, c), device_id_type=MESH)

    @pl.when(z > 0)
    def _():
        pl.semaphore_signal(barrier, inc=1, device_id=(r - CORES, c), device_id_type=MESH)

    first_row = (r * col_count + c) * width
    first_slot = first_row // B
    slot_count = lookup_ref.shape[0]
    slot_of_row = (first_row + lax.broadcasted_iota(jnp.int32, (width, order), 0)) // B
    for panel in range(2):
        which = sequence_ref[panel]
        kept = jnp.zeros((width, order), jnp.int32)
        for step in range((width + B - 2) // B + 1):
            slot = jnp.minimum(first_slot + step, slot_count - 1)
            flag = pattern_ref[which, lookup_ref[slot]]
            kept = jnp.where(slot_of_row == first_slot + step, flag, kept)
        values = panels_ref[which].astype(F32)
        row_rows[c, panel] = jnp.where(kept == 1, values, 0.0).astype(BF16)

    neighbours = col_count + (z < last_z).astype(jnp.int32) + (z > 0).astype(jnp.int32)
    pl.semaphore_wait(barrier, neighbours)

    def row_copy(step):
        target = (r + step) % col_count
        return target != c, pltpu.make_async_remote_copy(
            src_ref=row_rows.at[c], dst_ref=row_rows.at[c],
            send_sem=row_send.at[step], recv_sem=row_recv.at[c],
            device_id=(r, target), device_id_type=MESH,
        )

    def row_wait(piece):
        pltpu.make_async_remote_copy(
            src_ref=row_rows.at[piece], dst_ref=row_rows.at[piece],
            send_sem=row_send.at[0], recv_sem=row_recv.at[piece],
            device_id=(r, c), device_id_type=MESH,
        ).wait_recv()

    def col_copy(step, panel, way, target):
        piece = (c + step) % col_count
        chunk = 2 * step + panel
        return pltpu.make_async_remote_copy(
            src_ref=col_rows.at[piece, panel], dst_ref=col_rows.at[piece, panel],
            send_sem=col_send.at[way, chunk], recv_sem=col_recv.at[chunk],
            device_id=(target, c), device_id_type=MESH,
        )

    for step in range(col_count):
        wanted, copy = row_copy(step)
        pl.when(wanted)(copy.start)

    def forward(step, panel):
        piece = (c + step) % col_count

        @pl.when(is_source)
        def _():
            if step > 0 and panel == 0:
                row_wait(piece)
            col_rows[piece, panel] = row_rows[piece, panel]

        @pl.when(jnp.logical_not(is_source))
        def _():
            col_copy(step, panel, 0, sibling).wait_recv()

        for way, (wanted, target) in enumerate(sends):
            pl.when(wanted)(col_copy(step, panel, way, target).start)

    chunks = [(step, panel) for step in range(col_count) for panel in range(2)]
    turn = iter(chunks)
    ticks = iter(range(1, 1000))
    share = -(-len(chunks) // 8)

    def relay():
        if next(ticks) % 3 == 0:
            for _ in range(share):
                chunk = next(turn, None)
                if chunk is not None:
                    pl.when(main)(functools.partial(forward, *chunk))

    a_ref[...] = diagonals_ref[sequence_ref[0]]
    k = coupling_ref[...].astype(F32)
    k_ref[...] = jnp.where(sequence_ref[0] == 1, k.T, k).astype(BF16)
    open_inverse(a_ref, w_ref, f_ref, x_ref, relay)
    cubic_inverse(a_ref, w_ref, f_ref, x_ref, y_ref, relay)
    total = close_inverse(a_ref, None, w_ref, f_ref, first_ref, low_ref, relay)
    link_ref[...] = solved(k_ref[...], first_ref, low_ref).astype(BF16)
    relay()
    shrunk = diagonals_ref[sequence_ref[1]].astype(F32) - nt(link_ref[...], link_ref[...])
    a_ref[...], rest_ref[...] = split(shrunk)
    relay()
    open_inverse(a_ref, w_ref, f_ref, x_ref, relay)
    cubic_inverse(a_ref, w_ref, f_ref, x_ref, y_ref, relay)
    cubic_inverse(a_ref, w_ref, f_ref, x_ref, y_ref, relay)
    for chunk in turn:
        pl.when(main)(functools.partial(forward, *chunk))
    total = jnp.maximum(total, close_inverse(a_ref, rest_ref, w_ref, f_ref, second_ref, last_ref, lambda: None))
    residual_ref[...] = jnp.broadcast_to(jnp.sum(total, axis=1, keepdims=True), residual_ref.shape)

    for step in range(1, col_count):
        pl.when(jnp.logical_not(is_source))(functools.partial(row_wait, (c + step) % col_count))
    row_keep = pltpu.make_async_copy(row_rows, row_out, out_sem.at[0])
    row_keep.start()
    rows = pieces(row_rows)
    lead(rows, row_factor, first_ref, low_ref)
    follow(rows, row_factor, link_ref, second_ref, last_ref)
    write_factor(row_factor, factor_ref, sequence_ref, c)
    for chunk in chunks:
        pl.when(jnp.logical_not(main))(functools.partial(forward, *chunk))
    col_keep = pltpu.make_async_copy(col_rows, col_out, out_sem.at[1])
    col_keep.start()
    rows = pieces(col_rows)
    lead(rows, col_factor, first_ref, low_ref)
    follow(rows, col_factor, link_ref, second_ref, last_ref)

    fetch.wait()
    write_updated(row_factor, col_factor, held, updated_ref)
    row_keep.wait()
    col_keep.wait()
    for step in range(col_count):
        wanted, copy = row_copy(step)
        pl.when(wanted)(copy.wait_send)
    for step, panel in chunks:
        for way, (wanted, target) in enumerate(sends):
            pl.when(wanted)(col_copy(step, panel, way, target).wait_send)


def local(col_count, row_count, trailing, panels, diagonals, coupling, pattern, lookup, sequence):
    width, order = panels.shape[1], panels.shape[2]
    rows, columns = trailing.shape
    vmem = pl.BlockSpec(memory_space=pltpu.VMEM)
    smem = pl.BlockSpec(memory_space=pltpu.SMEM)
    square = (order, order)
    rest = (trailing, panels, diagonals, coupling, pattern, lookup, sequence)
    gathered = (col_count, 2, width, order)
    updated, factor, residual, row_rows, col_rows = pl.pallas_call(
        functools.partial(kernel, col_count, row_count),
        out_shape=(
            jax.ShapeDtypeStruct(trailing.shape, BF16),
            jax.ShapeDtypeStruct(panels.shape, BF16),
            jax.ShapeDtypeStruct((8, 128), F32),
            jax.ShapeDtypeStruct(gathered, BF16),
            jax.ShapeDtypeStruct(gathered, BF16),
        ),
        in_specs=[pl.BlockSpec(memory_space=pl.ANY), vmem, vmem, vmem, smem, smem, smem],
        out_specs=(vmem, vmem, vmem, pl.BlockSpec(memory_space=pl.ANY), pl.BlockSpec(memory_space=pl.ANY)),
        scratch_shapes=[
            pltpu.VMEM((col_count, 2, width, order), BF16),
            pltpu.VMEM((col_count, 2, width, order), BF16),
            pltpu.VMEM(square, BF16), pltpu.VMEM(square, BF16), pltpu.VMEM(square, BF16),
            pltpu.VMEM(square, BF16), pltpu.VMEM(square, BF16), pltpu.VMEM(square, BF16),
            pltpu.VMEM(square, BF16),
            pltpu.VMEM(square, BF16), pltpu.VMEM(square, BF16), pltpu.VMEM(square, BF16),
            pltpu.VMEM(square, BF16), pltpu.VMEM(square, BF16),
            pltpu.VMEM((rows, 2 * order), BF16), pltpu.VMEM((columns, 2 * order), BF16),
            pltpu.VMEM((rows, columns), BF16),
            pltpu.SemaphoreType.DMA((col_count,)), pltpu.SemaphoreType.DMA((col_count,)),
            pltpu.SemaphoreType.DMA((3, 2 * col_count)), pltpu.SemaphoreType.DMA((2 * col_count,)),
            pltpu.SemaphoreType.DMA, pltpu.SemaphoreType.DMA((2,)),
        ],
        compiler_params=pltpu.CompilerParams(
            collective_id=0, has_side_effects=True, vmem_limit_bytes=48 * 2**20
        ),
        cost_estimate=pl.CostEstimate(flops=10**10, bytes_accessed=6 * 10**6, transcendentals=0),
    )(*rest)
    slow = pl.pallas_call(
        slow_kernel,
        out_shape=(
            jax.ShapeDtypeStruct(trailing.shape, BF16),
            jax.ShapeDtypeStruct(panels.shape, BF16),
        ),
        in_specs=[vmem, vmem, vmem, vmem, vmem, smem],
        out_specs=(vmem, vmem),
        scratch_shapes=[pltpu.VMEM(square, F32), pltpu.VMEM(square, F32)]
        + [pltpu.VMEM(square, BF16)] * 6
        + [pltpu.VMEM((rows, 2 * order), BF16), pltpu.VMEM((columns, 2 * order), BF16)],
        compiler_params=pltpu.CompilerParams(vmem_limit_bytes=48 * 2**20),
    )
    return lax.cond(
        residual[0, 0] < TOLERANCE,
        lambda *_: (updated, factor),
        lambda *args: tuple(slow(*args)),
        trailing, row_rows, col_rows, diagonals, coupling, sequence,
    )


def solution(mesh):
    return jax.shard_map(
        functools.partial(local, mesh.shape["col"], mesh.shape["row"]),
        mesh=mesh,
        in_specs=(P("row", "col"), P(None, ("row", "col"), None), P(), P(), P(), P(), P()),
        out_specs=(P("row", "col"), P(None, ("row", "col"), None)),
        check_vma=False,
    )
```

```python
import functools

import jax
import jax.numpy as jnp
from jax import lax
from jax.experimental import pallas as pl
from jax.experimental.pallas import tpu as pltpu
from jax.sharding import PartitionSpec as P

B = 128
CORES = 2
MESH = pl.DeviceIdType.MESH
TOLERANCE = 0.01
F32 = jnp.float32
BF16 = jnp.bfloat16


def nt(left, right):
    return lax.dot_general(left, right, (((1,), (1,)), ((), ())), preferred_element_type=F32)


def nn(left, right):
    return lax.dot_general(left, right, (((1,), (0,)), ((), ())), preferred_element_type=F32)


def split(value):
    high = value.astype(BF16)
    return high, (value - high.astype(F32)).astype(BF16)


def blocks(order):
    size = 256 if order % 256 == 0 else order
    return size, order // size


def place(index, size):
    return pl.ds(index * size, size)


def ramp(index, size):
    return pl.ds(0, (index + 1) * size)


def on_diagonal(size):
    row = lax.broadcasted_iota(jnp.int32, (size, size), 0)
    column = lax.broadcasted_iota(jnp.int32, (size, size), 1)
    return row, column


def lower_half(value, i, j):
    if j < i:
        return value
    row, column = on_diagonal(value.shape[0])
    return jnp.where(column < row, value, jnp.where(column == row, 0.5 * value, 0.0))


def less_identity(value, i, j):
    if j < i:
        return value
    row, column = on_diagonal(value.shape[0])
    return value - jnp.where(row == column, 1.0, 0.0)


def correct(f_ref, x_ref, tick):
    size, count = blocks(f_ref.shape[0])
    for i in range(count):
        for j in range(i + 1):
            square = nt(f_ref[place(i, size), ramp(j, size)], f_ref[place(j, size), ramp(j, size)])
            f = f_ref[place(i, size), place(j, size)].astype(F32)
            x_ref[place(i, size), place(j, size)] = (f - lower_half(square, i, j)).astype(BF16)
        tick()


def lower_product(x_ref, y_ref, i, j, size):
    middle = pl.ds(j * size, (i - j + 1) * size)
    return nn(x_ref[place(i, size), middle], y_ref[middle, place(j, size)])


def open_inverse(a_ref, w_ref, f_ref, x_ref, tick):
    size, count = blocks(a_ref.shape[0])
    row, column = on_diagonal(size)
    across = []
    for i in range(count):
        a = a_ref[place(i, size), place(i, size)].astype(F32)
        diagonal = jnp.where(row == column, a, 0.0)
        down = lax.rsqrt(jnp.sum(diagonal, axis=1, keepdims=True))
        across.append(lax.rsqrt(jnp.sum(diagonal, axis=0, keepdims=True)))
        for j in range(i + 1):
            f = a_ref[place(i, size), place(j, size)].astype(F32) * down * across[j]
            if i == j:
                f = jnp.where(column < row, f, 0.0)
            f_ref[place(i, size), place(j, size)] = f.astype(BF16)
    correct(f_ref, x_ref, tick)
    for i in range(count):
        for j in range(i + 1):
            x = x_ref[place(i, size), place(j, size)].astype(F32)
            new = lower_product(x_ref, x_ref, i, j, size) - x
            if i == j:
                new = new + jnp.where(row == column, 1.0, 0.0)
            w_ref[place(i, size), place(j, size)] = (new * across[j]).astype(BF16)
        tick()


def cubic_inverse(a_ref, w_ref, f_ref, x_ref, y_ref, tick):
    size, count = blocks(a_ref.shape[0])
    for i in range(count):
        own = ramp(i, size)
        image = nn(w_ref[place(i, size), own], a_ref[own, own]).astype(BF16)
        for j in range(i + 1):
            square = nt(image[:, : (j + 1) * size], w_ref[place(j, size), ramp(j, size)])
            f = lower_half(less_identity(square, i, j), i, j)
            f_ref[place(i, size), place(j, size)] = f.astype(BF16)
        tick()
    correct(f_ref, x_ref, tick)
    for i in range(count):
        for j in range(i + 1):
            y_ref[place(i, size), place(j, size)] = lower_product(x_ref, w_ref, i, j, size).astype(BF16)
        tick()
    for i in range(count):
        for j in range(i + 1):
            spot = place(i, size), place(j, size)
            change = lower_product(x_ref, y_ref, i, j, size) - y_ref[spot].astype(F32)
            w_ref[spot] = (w_ref[spot].astype(F32) + change).astype(BF16)
        tick()


def close_inverse(a_ref, rest_ref, w_ref, f_ref, high_ref, low_ref, tick):
    size, count = blocks(a_ref.shape[0])
    total = jnp.zeros((1, size), F32)
    for i in range(count):
        own = ramp(i, size)
        image = nn(w_ref[place(i, size), own], a_ref[own, own])
        if rest_ref is not None:
            image = image + nn(w_ref[place(i, size), own], rest_ref[own, own])
        high, low = split(image)
        for j in range(i + 1):
            far = (j + 1) * size
            beside = w_ref[place(j, size), ramp(j, size)]
            square = nt(high[:, :far], beside) + nt(low[:, :far], beside)
            f = lower_half(less_identity(square, i, j), i, j)
            total = total + jnp.sum(f * f, axis=0, keepdims=True)
            f_ref[place(i, size), place(j, size)] = f.astype(BF16)
        tick()
    for i in range(count):
        for j in range(i + 1):
            spot = place(i, size), place(j, size)
            new = w_ref[spot].astype(F32) - lower_product(f_ref, w_ref, i, j, size)
            high_ref[spot], low_ref[spot] = split(new)
        tick()
    return total


def solved(high, high_ref, low_ref, low=None):
    size, count = blocks(high_ref.shape[0])
    parts = []
    for j in range(count):
        far = (j + 1) * size
        beside = high_ref[place(j, size), ramp(j, size)]
        part = nt(high[:, :far], beside) + nt(high[:, :far], low_ref[place(j, size), ramp(j, size)])
        if low is not None:
            part = part + nt(low[:, :far], beside)
        parts.append(part)
    return jnp.concatenate(parts, axis=1) if count > 1 else parts[0]


def lead(rows, factors, first_ref, low_ref):
    order = first_ref.shape[0]
    factors[:, :order] = solved(rows[0], first_ref, low_ref).astype(BF16)


def follow(rows, factors, link_ref, second_ref, rest_ref):
    order = link_ref.shape[0]
    rest = rows[1].astype(F32) - nt(factors[:, :order], link_ref[...])
    high, low = split(rest)
    factors[:, order:] = solved(high, second_ref, rest_ref, low).astype(BF16)


def pieces(ref):
    count, _, width, order = ref.shape
    return [ref[:, panel].reshape(count * width, order) for panel in range(2)]


def write_factor(row_factor, factor_ref, sequence_ref, c):
    width, order = factor_ref.shape[1], factor_ref.shape[2]
    own = row_factor[pl.ds(pl.multiple_of(c * width, 16), width), :]
    swapped = sequence_ref[0] == 1
    mine = own[:, :order].astype(F32), own[:, order:].astype(F32)
    factor_ref[0] = jnp.where(swapped, mine[1], mine[0]).astype(BF16)
    factor_ref[1] = jnp.where(swapped, mine[0], mine[1]).astype(BF16)


def write_updated(row_factor, col_factor, held, updated_ref):
    height = held.shape[0]
    for start in range(0, height, 256):
        part = pl.ds(start, min(256, height - start))
        change = nt(row_factor[part, :], col_factor[...])
        updated_ref[part, :] = (held[part, :].astype(F32) - change).astype(BF16)


def eliminate(a_ref, w_ref, high_ref, low_ref):
    order = a_ref.shape[0]
    row = lax.broadcasted_iota(jnp.int32, (order, order), 0)
    column = lax.broadcasted_iota(jnp.int32, (order, order), 1)
    w_ref[...] = jnp.where(row == column, 1.0, 0.0)

    def step(j, carry):
        pivot_row = a_ref[pl.ds(j, 1), :]
        lane = lax.broadcasted_iota(jnp.int32, (1, order), 1)
        pivot = jnp.sum(jnp.where(lane == j, pivot_row, 0.0), axis=1, keepdims=True)
        scale = lax.rsqrt(pivot)
        pivot_row = pivot_row * scale
        done = w_ref[pl.ds(j, 1), :] * scale
        a = a_ref[...]
        below = jnp.sum(jnp.where(column == j, a, 0.0), axis=1, keepdims=True) * scale
        below = jnp.where(row[:, :1] > j, below, 0.0)
        a_ref[...] = a - below * pivot_row
        w_ref[...] = w_ref[...] - below * done
        w_ref[pl.ds(j, 1), :] = done
        return carry

    lax.fori_loop(0, order, step, 0)
    high_ref[...], low_ref[...] = split(w_ref[...])


def slow_kernel(
    trailing_ref, row_rows, col_rows, diagonals_ref, coupling_ref, sequence_ref,
    updated_ref, factor_ref,
    a_ref, w_ref, k_ref, first_ref, low_ref, link_ref, second_ref, rest_ref, row_factor, col_factor,
):
    a_ref[...] = diagonals_ref[sequence_ref[0]].astype(F32)
    k = coupling_ref[...].astype(F32)
    k_ref[...] = jnp.where(sequence_ref[0] == 1, k.T, k).astype(BF16)
    eliminate(a_ref, w_ref, first_ref, low_ref)
    link_ref[...] = solved(k_ref[...], first_ref, low_ref).astype(BF16)
    a_ref[...] = diagonals_ref[sequence_ref[1]].astype(F32) - nt(link_ref[...], link_ref[...])
    eliminate(a_ref, w_ref, second_ref, rest_ref)
    for rows, factors in ((row_rows, row_factor), (col_rows, col_factor)):
        lead(pieces(rows), factors, first_ref, low_ref)
        follow(pieces(rows), factors, link_ref, second_ref, rest_ref)
    write_factor(row_factor, factor_ref, sequence_ref, lax.axis_index("col"))
    write_updated(row_factor, col_factor, trailing_ref, updated_ref)


def kernel(
    col_count, row_count,
    trailing_ref, panels_ref, diagonals_ref, coupling_ref, pattern_ref, lookup_ref, sequence_ref,
    updated_ref, factor_ref, residual_ref, row_out, col_out,
    row_rows, col_rows, a_ref, rest_ref, k_ref, w_ref, f_ref, x_ref, y_ref,
    first_ref, low_ref, link_ref, second_ref, last_ref, row_factor, col_factor, held,
    row_send, row_recv, col_send, col_recv, held_sem, out_sem,
):
    r = lax.axis_index("row")
    c = lax.axis_index("col")
    width, order = panels_ref.shape[1], panels_ref.shape[2]
    z, source_z, last_z = r // CORES, c // CORES, row_count // CORES - 1
    main = r % CORES == c % CORES
    sibling = z * CORES + (CORES - 1 - r % CORES)
    is_source = r == c
    sends = (
        (main & (z >= source_z) & (z < last_z), jnp.minimum(r + CORES, row_count - 1)),
        (main & (z <= source_z) & (z > 0), jnp.maximum(r - CORES, 0)),
        (main, sibling),
    )

    fetch = pltpu.make_async_copy(trailing_ref, held, held_sem)
    fetch.start()

    barrier = pltpu.get_barrier_semaphore()
    for step in range(1, col_count):
        pl.semaphore_signal(barrier, inc=1, device_id=(r, (c + step) % col_count), device_id_type=MESH)
    pl.semaphore_signal(barrier, inc=1, device_id=(sibling, c), device_id_type=MESH)

    @pl.when(z < last_z)
    def _():
        pl.semaphore_signal(barrier, inc=1, device_id=(r + CORES, c), device_id_type=MESH)

    @pl.when(z > 0)
    def _():
        pl.semaphore_signal(barrier, inc=1, device_id=(r - CORES, c), device_id_type=MESH)

    first_row = (r * col_count + c) * width
    first_slot = first_row // B
    slot_count = lookup_ref.shape[0]
    slot_of_row = (first_row + lax.broadcasted_iota(jnp.int32, (width, order), 0)) // B
    for panel in range(2):
        which = sequence_ref[panel]
        kept = jnp.zeros((width, order), jnp.int32)
        for step in range((width + B - 2) // B + 1):
            slot = jnp.minimum(first_slot + step, slot_count - 1)
            flag = pattern_ref[which, lookup_ref[slot]]
            kept = jnp.where(slot_of_row == first_slot + step, flag, kept)
        values = panels_ref[which].astype(F32)
        row_rows[c, panel] = jnp.where(kept == 1, values, 0.0).astype(BF16)

    neighbours = col_count + (z < last_z).astype(jnp.int32) + (z > 0).astype(jnp.int32)
    pl.semaphore_wait(barrier, neighbours)

    def row_copy(step):
        target = (r + step) % col_count
        return target != c, pltpu.make_async_remote_copy(
            src_ref=row_rows.at[c], dst_ref=row_rows.at[c],
            send_sem=row_send.at[step], recv_sem=row_recv.at[c],
            device_id=(r, target), device_id_type=MESH,
        )

    def row_wait(piece):
        pltpu.make_async_remote_copy(
            src_ref=row_rows.at[piece], dst_ref=row_rows.at[piece],
            send_sem=row_send.at[0], recv_sem=row_recv.at[piece],
            device_id=(r, c), device_id_type=MESH,
        ).wait_recv()

    def col_copy(step, panel, way, target):
        piece = (c + step) % col_count
        chunk = 2 * step + panel
        return pltpu.make_async_remote_copy(
            src_ref=col_rows.at[piece, panel], dst_ref=col_rows.at[piece, panel],
            send_sem=col_send.at[way, chunk], recv_sem=col_recv.at[chunk],
            device_id=(target, c), device_id_type=MESH,
        )

    def send_row(step):
        wanted, copy = row_copy(step)
        pl.when(wanted)(copy.start)

    send_row(0)

    def forward(step, panel, from_source):
        piece = (c + step) % col_count
        if from_source:
            if step > 0 and panel == 0:
                row_wait(piece)
            col_rows[piece, panel] = row_rows[piece, panel]
        else:
            col_copy(step, panel, 0, sibling).wait_recv()
        for way, (wanted, target) in enumerate(sends):
            pl.when(wanted)(col_copy(step, panel, way, target).start)

    chunks = [(step, panel) for step in range(col_count) for panel in range(2)]
    share = -(-len(chunks) // 8)
    groups = [chunks[start : start + share] for start in range(0, len(chunks), share)]
    farthest = min(row_count // CORES - 1, 3)
    away = jnp.minimum(jnp.abs(z - source_z), farthest)
    plan = {distance: list(enumerate(groups)) for distance in range(farthest + 1)}
    ticks = iter(range(1, 1000))

    def relay_group(distance, group):
        @pl.when(main & (away == distance))
        def _():
            for step, panel in group:
                forward(step, panel, distance == 0)

    def relay():
        tick = next(ticks)
        for distance, rest in plan.items():
            if rest and tick == 3 + 3 * rest[0][0] + 5 * distance:
                relay_group(distance, rest.pop(0)[1])
        for step in range(1, col_count):
            if tick == min(4 * step, 12):
                send_row(step)

    def finish_relays():
        for distance, rest in plan.items():
            while rest:
                relay_group(distance, rest.pop(0)[1])

    a_ref[...] = diagonals_ref[sequence_ref[0]]
    k = coupling_ref[...].astype(F32)
    k_ref[...] = jnp.where(sequence_ref[0] == 1, k.T, k).astype(BF16)
    open_inverse(a_ref, w_ref, f_ref, x_ref, relay)
    cubic_inverse(a_ref, w_ref, f_ref, x_ref, y_ref, relay)
    total = close_inverse(a_ref, None, w_ref, f_ref, first_ref, low_ref, relay)
    link_ref[...] = solved(k_ref[...], first_ref, low_ref).astype(BF16)
    relay()
    shrunk = diagonals_ref[sequence_ref[1]].astype(F32) - nt(link_ref[...], link_ref[...])
    a_ref[...], rest_ref[...] = split(shrunk)
    relay()
    open_inverse(a_ref, w_ref, f_ref, x_ref, relay)
    cubic_inverse(a_ref, w_ref, f_ref, x_ref, y_ref, relay)
    cubic_inverse(a_ref, w_ref, f_ref, x_ref, y_ref, relay)
    total = jnp.maximum(total, close_inverse(a_ref, rest_ref, w_ref, f_ref, second_ref, last_ref, relay))
    finish_relays()
    residual_ref[...] = jnp.broadcast_to(jnp.sum(total, axis=1, keepdims=True), residual_ref.shape)

    for step in range(1, col_count):
        pl.when(jnp.logical_not(is_source))(functools.partial(row_wait, (c + step) % col_count))
    row_keep = pltpu.make_async_copy(row_rows, row_out, out_sem.at[0])
    row_keep.start()
    rows = pieces(row_rows)
    lead(rows, row_factor, first_ref, low_ref)
    follow(rows, row_factor, link_ref, second_ref, last_ref)
    write_factor(row_factor, factor_ref, sequence_ref, c)
    for step in range(col_count):
        piece = (c + step) % col_count

        @pl.when(jnp.logical_not(main))
        def _():
            for panel in range(2):
                col_copy(step, panel, 0, sibling).wait_recv()

        here = pl.ds(pl.multiple_of(piece * width, 16), width)
        rows = col_rows[piece, 0], col_rows[piece, 1]
        leading = solved(rows[0], first_ref, low_ref).astype(BF16)
        col_factor[here, :order] = leading
        rest = rows[1].astype(F32) - nt(leading, link_ref[...])
        high, low = split(rest)
        col_factor[here, order:] = solved(high, second_ref, last_ref, low).astype(BF16)
    col_keep = pltpu.make_async_copy(col_rows, col_out, out_sem.at[1])
    col_keep.start()

    fetch.wait()
    write_updated(row_factor, col_factor, held, updated_ref)
    row_keep.wait()
    col_keep.wait()
    for step in range(col_count):
        wanted, copy = row_copy(step)
        pl.when(wanted)(copy.wait_send)
    for step, panel in chunks:
        for way, (wanted, target) in enumerate(sends):
            pl.when(wanted)(col_copy(step, panel, way, target).wait_send)


def local(col_count, row_count, trailing, panels, diagonals, coupling, pattern, lookup, sequence):
    width, order = panels.shape[1], panels.shape[2]
    rows, columns = trailing.shape
    vmem = pl.BlockSpec(memory_space=pltpu.VMEM)
    smem = pl.BlockSpec(memory_space=pltpu.SMEM)
    square = (order, order)
    rest = (trailing, panels, diagonals, coupling, pattern, lookup, sequence)
    gathered = (col_count, 2, width, order)
    updated, factor, residual, row_rows, col_rows = pl.pallas_call(
        functools.partial(kernel, col_count, row_count),
        out_shape=(
            jax.ShapeDtypeStruct(trailing.shape, BF16),
            jax.ShapeDtypeStruct(panels.shape, BF16),
            jax.ShapeDtypeStruct((8, 128), F32),
            jax.ShapeDtypeStruct(gathered, BF16),
            jax.ShapeDtypeStruct(gathered, BF16),
        ),
        in_specs=[pl.BlockSpec(memory_space=pl.ANY), vmem, vmem, vmem, smem, smem, smem],
        out_specs=(vmem, vmem, vmem, pl.BlockSpec(memory_space=pl.ANY), pl.BlockSpec(memory_space=pl.ANY)),
        scratch_shapes=[
            pltpu.VMEM((col_count, 2, width, order), BF16),
            pltpu.VMEM((col_count, 2, width, order), BF16),
            pltpu.VMEM(square, BF16), pltpu.VMEM(square, BF16), pltpu.VMEM(square, BF16),
            pltpu.VMEM(square, BF16), pltpu.VMEM(square, BF16), pltpu.VMEM(square, BF16),
            pltpu.VMEM(square, BF16),
            pltpu.VMEM(square, BF16), pltpu.VMEM(square, BF16), pltpu.VMEM(square, BF16),
            pltpu.VMEM(square, BF16), pltpu.VMEM(square, BF16),
            pltpu.VMEM((rows, 2 * order), BF16), pltpu.VMEM((columns, 2 * order), BF16),
            pltpu.VMEM((rows, columns), BF16),
            pltpu.SemaphoreType.DMA((col_count,)), pltpu.SemaphoreType.DMA((col_count,)),
            pltpu.SemaphoreType.DMA((3, 2 * col_count)), pltpu.SemaphoreType.DMA((2 * col_count,)),
            pltpu.SemaphoreType.DMA, pltpu.SemaphoreType.DMA((2,)),
        ],
        compiler_params=pltpu.CompilerParams(
            collective_id=0, has_side_effects=True, vmem_limit_bytes=60 * 2**20
        ),
        cost_estimate=pl.CostEstimate(flops=10**10, bytes_accessed=6 * 10**6, transcendentals=0),
    )(*rest)
    slow = pl.pallas_call(
        slow_kernel,
        out_shape=(
            jax.ShapeDtypeStruct(trailing.shape, BF16),
            jax.ShapeDtypeStruct(panels.shape, BF16),
        ),
        in_specs=[vmem, vmem, vmem, vmem, vmem, smem],
        out_specs=(vmem, vmem),
        scratch_shapes=[pltpu.VMEM(square, F32), pltpu.VMEM(square, F32)]
        + [pltpu.VMEM(square, BF16)] * 6
        + [pltpu.VMEM((rows, 2 * order), BF16), pltpu.VMEM((columns, 2 * order), BF16)],
        compiler_params=pltpu.CompilerParams(vmem_limit_bytes=48 * 2**20),
    )
    return lax.cond(
        residual[0, 0] < TOLERANCE,
        lambda *_: (updated, factor),
        lambda *args: tuple(slow(*args)),
        trailing, row_rows, col_rows, diagonals, coupling, sequence,
    )


def solution(mesh):
    return jax.shard_map(
        functools.partial(local, mesh.shape["col"], mesh.shape["row"]),
        mesh=mesh,
        in_specs=(P("row", "col"), P(None, ("row", "col"), None), P(), P(), P(), P(), P()),
        out_specs=(P("row", "col"), P(None, ("row", "col"), None)),
        check_vma=False,
    )
```

```python
import functools

import jax
import jax.numpy as jnp
from jax import lax
from jax.experimental import pallas as pl
from jax.experimental.pallas import tpu as pltpu
from jax.sharding import PartitionSpec as P

B = 128
CORES = 2
MESH = pl.DeviceIdType.MESH
TOLERANCE = 0.01
F32 = jnp.float32
BF16 = jnp.bfloat16


def nt(left, right):
    return lax.dot_general(left, right, (((1,), (1,)), ((), ())), preferred_element_type=F32)


def nn(left, right):
    return lax.dot_general(left, right, (((1,), (0,)), ((), ())), preferred_element_type=F32)


def split(value):
    high = value.astype(BF16)
    return high, (value - high.astype(F32)).astype(BF16)


def blocks(order):
    size = 256 if order % 256 == 0 else order
    return size, order // size


def place(index, size):
    return pl.ds(index * size, size)


def ramp(index, size):
    return pl.ds(0, (index + 1) * size)


def on_diagonal(size):
    row = lax.broadcasted_iota(jnp.int32, (size, size), 0)
    column = lax.broadcasted_iota(jnp.int32, (size, size), 1)
    return row, column


def lower_half(value, i, j):
    if j < i:
        return value
    row, column = on_diagonal(value.shape[0])
    return jnp.where(column < row, value, jnp.where(column == row, 0.5 * value, 0.0))


def less_identity(value, i, j):
    if j < i:
        return value
    row, column = on_diagonal(value.shape[0])
    return value - jnp.where(row == column, 1.0, 0.0)


def correct(f_ref, x_ref, tick):
    size, count = blocks(f_ref.shape[0])
    for i in range(count):
        for j in range(i + 1):
            square = nt(f_ref[place(i, size), ramp(j, size)], f_ref[place(j, size), ramp(j, size)])
            f = f_ref[place(i, size), place(j, size)].astype(F32)
            x_ref[place(i, size), place(j, size)] = (f - lower_half(square, i, j)).astype(BF16)
        tick()


def lower_product(x_ref, y_ref, i, j, size):
    middle = pl.ds(j * size, (i - j + 1) * size)
    return nn(x_ref[place(i, size), middle], y_ref[middle, place(j, size)])


def open_inverse(a_ref, w_ref, f_ref, x_ref, tick):
    size, count = blocks(a_ref.shape[0])
    row, column = on_diagonal(size)
    across = []
    for i in range(count):
        a = a_ref[place(i, size), place(i, size)].astype(F32)
        diagonal = jnp.where(row == column, a, 0.0)
        down = lax.rsqrt(jnp.sum(diagonal, axis=1, keepdims=True))
        across.append(lax.rsqrt(jnp.sum(diagonal, axis=0, keepdims=True)))
        for j in range(i + 1):
            f = a_ref[place(i, size), place(j, size)].astype(F32) * down * across[j]
            if i == j:
                f = jnp.where(column < row, f, 0.0)
            f_ref[place(i, size), place(j, size)] = f.astype(BF16)
    correct(f_ref, x_ref, tick)
    for i in range(count):
        for j in range(i + 1):
            x = x_ref[place(i, size), place(j, size)].astype(F32)
            new = lower_product(x_ref, x_ref, i, j, size) - x
            if i == j:
                new = new + jnp.where(row == column, 1.0, 0.0)
            w_ref[place(i, size), place(j, size)] = (new * across[j]).astype(BF16)
        tick()


def cubic_inverse(a_ref, w_ref, f_ref, x_ref, y_ref, tick):
    size, count = blocks(a_ref.shape[0])
    for i in range(count):
        own = ramp(i, size)
        image = nn(w_ref[place(i, size), own], a_ref[own, own]).astype(BF16)
        for j in range(i + 1):
            square = nt(image[:, : (j + 1) * size], w_ref[place(j, size), ramp(j, size)])
            f = lower_half(less_identity(square, i, j), i, j)
            f_ref[place(i, size), place(j, size)] = f.astype(BF16)
        tick()
    correct(f_ref, x_ref, tick)
    for i in range(count):
        for j in range(i + 1):
            y_ref[place(i, size), place(j, size)] = lower_product(x_ref, w_ref, i, j, size).astype(BF16)
        tick()
    for i in range(count):
        for j in range(i + 1):
            spot = place(i, size), place(j, size)
            change = lower_product(x_ref, y_ref, i, j, size) - y_ref[spot].astype(F32)
            w_ref[spot] = (w_ref[spot].astype(F32) + change).astype(BF16)
        tick()


def close_inverse(a_ref, rest_ref, w_ref, f_ref, high_ref, low_ref, tick):
    size, count = blocks(a_ref.shape[0])
    total = jnp.zeros((1, size), F32)
    for i in range(count):
        own = ramp(i, size)
        image = nn(w_ref[place(i, size), own], a_ref[own, own])
        if rest_ref is not None:
            image = image + nn(w_ref[place(i, size), own], rest_ref[own, own])
        high, low = split(image)
        for j in range(i + 1):
            far = (j + 1) * size
            beside = w_ref[place(j, size), ramp(j, size)]
            square = nt(high[:, :far], beside) + nt(low[:, :far], beside)
            f = lower_half(less_identity(square, i, j), i, j)
            total = total + jnp.sum(f * f, axis=0, keepdims=True)
            f_ref[place(i, size), place(j, size)] = f.astype(BF16)
        tick()
    for i in range(count):
        for j in range(i + 1):
            spot = place(i, size), place(j, size)
            new = w_ref[spot].astype(F32) - lower_product(f_ref, w_ref, i, j, size)
            high_ref[spot], low_ref[spot] = split(new)
        tick()
    return total


def solved(high, high_ref, low_ref, low=None):
    size, count = blocks(high_ref.shape[0])
    parts = []
    for j in range(count):
        far = (j + 1) * size
        beside = high_ref[place(j, size), ramp(j, size)]
        part = nt(high[:, :far], beside) + nt(high[:, :far], low_ref[place(j, size), ramp(j, size)])
        if low is not None:
            part = part + nt(low[:, :far], beside)
        parts.append(part)
    return jnp.concatenate(parts, axis=1) if count > 1 else parts[0]


def lead(rows, factors, first_ref, low_ref):
    order = first_ref.shape[0]
    factors[:, :order] = solved(rows[0], first_ref, low_ref).astype(BF16)


def follow(rows, factors, link_ref, second_ref, rest_ref):
    order = link_ref.shape[0]
    rest = rows[1].astype(F32) - nt(factors[:, :order], link_ref[...])
    high, low = split(rest)
    factors[:, order:] = solved(high, second_ref, rest_ref, low).astype(BF16)


def pieces(ref):
    count, _, width, order = ref.shape
    return [ref[:, panel].reshape(count * width, order) for panel in range(2)]


def write_factor(row_factor, factor_ref, sequence_ref, c):
    width, order = factor_ref.shape[1], factor_ref.shape[2]
    own = row_factor[pl.ds(pl.multiple_of(c * width, 16), width), :]
    swapped = sequence_ref[0] == 1
    mine = own[:, :order].astype(F32), own[:, order:].astype(F32)
    factor_ref[0] = jnp.where(swapped, mine[1], mine[0]).astype(BF16)
    factor_ref[1] = jnp.where(swapped, mine[0], mine[1]).astype(BF16)


def write_updated(row_factor, col_factor, held, updated_ref):
    height = held.shape[0]
    for start in range(0, height, 256):
        part = pl.ds(start, min(256, height - start))
        change = nt(row_factor[part, :], col_factor[...])
        updated_ref[part, :] = (held[part, :].astype(F32) - change).astype(BF16)


def eliminate(a_ref, w_ref, high_ref, low_ref):
    order = a_ref.shape[0]
    row = lax.broadcasted_iota(jnp.int32, (order, order), 0)
    column = lax.broadcasted_iota(jnp.int32, (order, order), 1)
    w_ref[...] = jnp.where(row == column, 1.0, 0.0)

    def step(j, carry):
        pivot_row = a_ref[pl.ds(j, 1), :]
        lane = lax.broadcasted_iota(jnp.int32, (1, order), 1)
        pivot = jnp.sum(jnp.where(lane == j, pivot_row, 0.0), axis=1, keepdims=True)
        scale = lax.rsqrt(pivot)
        pivot_row = pivot_row * scale
        done = w_ref[pl.ds(j, 1), :] * scale
        a = a_ref[...]
        below = jnp.sum(jnp.where(column == j, a, 0.0), axis=1, keepdims=True) * scale
        below = jnp.where(row[:, :1] > j, below, 0.0)
        a_ref[...] = a - below * pivot_row
        w_ref[...] = w_ref[...] - below * done
        w_ref[pl.ds(j, 1), :] = done
        return carry

    lax.fori_loop(0, order, step, 0)
    high_ref[...], low_ref[...] = split(w_ref[...])


def slow_kernel(
    trailing_ref, row_rows, col_rows, diagonals_ref, coupling_ref, sequence_ref,
    updated_ref, factor_ref,
    a_ref, w_ref, k_ref, first_ref, low_ref, link_ref, second_ref, rest_ref, row_factor, col_factor,
):
    a_ref[...] = diagonals_ref[sequence_ref[0]].astype(F32)
    k = coupling_ref[...].astype(F32)
    k_ref[...] = jnp.where(sequence_ref[0] == 1, k.T, k).astype(BF16)
    eliminate(a_ref, w_ref, first_ref, low_ref)
    link_ref[...] = solved(k_ref[...], first_ref, low_ref).astype(BF16)
    a_ref[...] = diagonals_ref[sequence_ref[1]].astype(F32) - nt(link_ref[...], link_ref[...])
    eliminate(a_ref, w_ref, second_ref, rest_ref)
    for rows, factors in ((row_rows, row_factor), (col_rows, col_factor)):
        lead(pieces(rows), factors, first_ref, low_ref)
        follow(pieces(rows), factors, link_ref, second_ref, rest_ref)
    write_factor(row_factor, factor_ref, sequence_ref, lax.axis_index("col"))
    write_updated(row_factor, col_factor, trailing_ref, updated_ref)


def kernel(
    col_count, row_count,
    trailing_ref, panels_ref, diagonals_ref, coupling_ref, pattern_ref, lookup_ref, sequence_ref,
    updated_ref, factor_ref, residual_ref, row_out, col_out,
    row_rows, col_rows, a_ref, rest_ref, k_ref, w_ref, f_ref, x_ref, y_ref,
    first_ref, low_ref, link_ref, second_ref, last_ref, row_factor, col_factor, held,
    row_send, row_recv, col_send, col_recv, held_sem, out_sem,
):
    r = lax.axis_index("row")
    c = lax.axis_index("col")
    width, order = panels_ref.shape[1], panels_ref.shape[2]
    z, source_z, last_z = r // CORES, c // CORES, row_count // CORES - 1
    main = r % CORES == c % CORES
    sibling = z * CORES + (CORES - 1 - r % CORES)
    is_source = r == c
    sends = (
        (main & (z >= source_z) & (z < last_z), jnp.minimum(r + CORES, row_count - 1)),
        (main & (z <= source_z) & (z > 0), jnp.maximum(r - CORES, 0)),
        (main, sibling),
    )

    fetch = pltpu.make_async_copy(trailing_ref, held, held_sem)
    fetch.start()

    barrier = pltpu.get_barrier_semaphore()
    for step in range(1, col_count):
        pl.semaphore_signal(barrier, inc=1, device_id=(r, (c + step) % col_count), device_id_type=MESH)
    pl.semaphore_signal(barrier, inc=1, device_id=(sibling, c), device_id_type=MESH)

    @pl.when(z < last_z)
    def _():
        pl.semaphore_signal(barrier, inc=1, device_id=(r + CORES, c), device_id_type=MESH)

    @pl.when(z > 0)
    def _():
        pl.semaphore_signal(barrier, inc=1, device_id=(r - CORES, c), device_id_type=MESH)

    first_row = (r * col_count + c) * width
    first_slot = first_row // B
    slot_count = lookup_ref.shape[0]
    slot_of_row = (first_row + lax.broadcasted_iota(jnp.int32, (width, order), 0)) // B
    for panel in range(2):
        which = sequence_ref[panel]
        kept = jnp.zeros((width, order), jnp.int32)
        for step in range((width + B - 2) // B + 1):
            slot = jnp.minimum(first_slot + step, slot_count - 1)
            flag = pattern_ref[which, lookup_ref[slot]]
            kept = jnp.where(slot_of_row == first_slot + step, flag, kept)
        values = panels_ref[which].astype(F32)
        row_rows[c, panel] = jnp.where(kept == 1, values, 0.0).astype(BF16)

    neighbours = col_count + (z < last_z).astype(jnp.int32) + (z > 0).astype(jnp.int32)
    pl.semaphore_wait(barrier, neighbours)

    def row_copy(step):
        target = (r + step) % col_count
        return target != c, pltpu.make_async_remote_copy(
            src_ref=row_rows.at[c], dst_ref=row_rows.at[c],
            send_sem=row_send.at[step], recv_sem=row_recv.at[c],
            device_id=(r, target), device_id_type=MESH,
        )

    def row_wait(piece):
        pltpu.make_async_remote_copy(
            src_ref=row_rows.at[piece], dst_ref=row_rows.at[piece],
            send_sem=row_send.at[0], recv_sem=row_recv.at[piece],
            device_id=(r, c), device_id_type=MESH,
        ).wait_recv()

    def col_copy(step, panel, way, target):
        piece = (c + step) % col_count
        chunk = 2 * step + panel
        return pltpu.make_async_remote_copy(
            src_ref=col_rows.at[piece, panel], dst_ref=col_rows.at[piece, panel],
            send_sem=col_send.at[way, chunk], recv_sem=col_recv.at[chunk],
            device_id=(target, c), device_id_type=MESH,
        )

    def send_row(step):
        wanted, copy = row_copy(step)
        pl.when(wanted)(copy.start)

    send_row(0)
    through = sends[0][0] | sends[1][0] | is_source

    def forward(step, panel, from_source):
        piece = (c + step) % col_count
        if from_source:
            if step > 0 and panel == 0:
                row_wait(piece)
            col_rows[piece, panel] = row_rows[piece, panel]
        else:
            col_copy(step, panel, 0, sibling).wait_recv()
        for way, (wanted, target) in enumerate(sends):
            pl.when(wanted)(col_copy(step, panel, way, target).start)

    chunks = [(step, panel) for step in range(col_count) for panel in range(2)]
    share = -(-len(chunks) // 8)
    groups = [chunks[start : start + share] for start in range(0, len(chunks), share)]
    farthest = min(row_count // CORES - 1, 3)
    away = jnp.minimum(jnp.abs(z - source_z), farthest)
    plan = {distance: list(enumerate(groups)) for distance in range(farthest + 1)}
    ticks = iter(range(1, 1000))

    def relay_group(distance, group):
        @pl.when(through & (away == distance))
        def _():
            for step, panel in group:
                forward(step, panel, distance == 0)

    def relay():
        tick = next(ticks)
        for distance, rest in plan.items():
            if rest and tick == 3 + 3 * rest[0][0] + 5 * distance:
                relay_group(distance, rest.pop(0)[1])
        for step in range(1, col_count):
            if tick == min(4 * step, 12):
                send_row(step)

    def finish_relays():
        for distance, rest in plan.items():
            while rest:
                relay_group(distance, rest.pop(0)[1])

    a_ref[...] = diagonals_ref[sequence_ref[0]]
    k = coupling_ref[...].astype(F32)
    k_ref[...] = jnp.where(sequence_ref[0] == 1, k.T, k).astype(BF16)
    open_inverse(a_ref, w_ref, f_ref, x_ref, relay)
    cubic_inverse(a_ref, w_ref, f_ref, x_ref, y_ref, relay)
    total = close_inverse(a_ref, None, w_ref, f_ref, first_ref, low_ref, relay)
    link_ref[...] = solved(k_ref[...], first_ref, low_ref).astype(BF16)
    relay()
    shrunk = diagonals_ref[sequence_ref[1]].astype(F32) - nt(link_ref[...], link_ref[...])
    a_ref[...], rest_ref[...] = split(shrunk)
    relay()
    open_inverse(a_ref, w_ref, f_ref, x_ref, relay)
    cubic_inverse(a_ref, w_ref, f_ref, x_ref, y_ref, relay)
    total = jnp.maximum(total, close_inverse(a_ref, rest_ref, w_ref, f_ref, second_ref, last_ref, relay))
    finish_relays()
    residual_ref[...] = jnp.broadcast_to(jnp.sum(total, axis=1, keepdims=True), residual_ref.shape)

    for step in range(1, col_count):
        pl.when(jnp.logical_not(is_source))(functools.partial(row_wait, (c + step) % col_count))
    row_keep = pltpu.make_async_copy(row_rows, row_out, out_sem.at[0])
    row_keep.start()
    rows = pieces(row_rows)
    lead(rows, row_factor, first_ref, low_ref)
    follow(rows, row_factor, link_ref, second_ref, last_ref)
    write_factor(row_factor, factor_ref, sequence_ref, c)
    for step in range(col_count):
        piece = (c + step) % col_count

        @pl.when(jnp.logical_not(main))
        def _():
            for panel in range(2):
                col_copy(step, panel, 0, sibling).wait_recv()

        @pl.when(main & jnp.logical_not(through))
        def _():
            for panel in range(2):
                forward(step, panel, False)

        here = pl.ds(pl.multiple_of(piece * width, 16), width)
        rows = col_rows[piece, 0], col_rows[piece, 1]
        leading = solved(rows[0], first_ref, low_ref).astype(BF16)
        col_factor[here, :order] = leading
        rest = rows[1].astype(F32) - nt(leading, link_ref[...])
        high, low = split(rest)
        col_factor[here, order:] = solved(high, second_ref, last_ref, low).astype(BF16)
    col_keep = pltpu.make_async_copy(col_rows, col_out, out_sem.at[1])
    col_keep.start()

    fetch.wait()
    write_updated(row_factor, col_factor, held, updated_ref)
    row_keep.wait()
    col_keep.wait()
    for step in range(col_count):
        wanted, copy = row_copy(step)
        pl.when(wanted)(copy.wait_send)
    for step, panel in chunks:
        for way, (wanted, target) in enumerate(sends):
            pl.when(wanted)(col_copy(step, panel, way, target).wait_send)


def local(col_count, row_count, trailing, panels, diagonals, coupling, pattern, lookup, sequence):
    width, order = panels.shape[1], panels.shape[2]
    rows, columns = trailing.shape
    vmem = pl.BlockSpec(memory_space=pltpu.VMEM)
    smem = pl.BlockSpec(memory_space=pltpu.SMEM)
    square = (order, order)
    rest = (trailing, panels, diagonals, coupling, pattern, lookup, sequence)
    gathered = (col_count, 2, width, order)
    updated, factor, residual, row_rows, col_rows = pl.pallas_call(
        functools.partial(kernel, col_count, row_count),
        out_shape=(
            jax.ShapeDtypeStruct(trailing.shape, BF16),
            jax.ShapeDtypeStruct(panels.shape, BF16),
            jax.ShapeDtypeStruct((8, 128), F32),
            jax.ShapeDtypeStruct(gathered, BF16),
            jax.ShapeDtypeStruct(gathered, BF16),
        ),
        in_specs=[pl.BlockSpec(memory_space=pl.ANY), vmem, vmem, vmem, smem, smem, smem],
        out_specs=(vmem, vmem, vmem, pl.BlockSpec(memory_space=pl.ANY), pl.BlockSpec(memory_space=pl.ANY)),
        scratch_shapes=[
            pltpu.VMEM((col_count, 2, width, order), BF16),
            pltpu.VMEM((col_count, 2, width, order), BF16),
            pltpu.VMEM(square, BF16), pltpu.VMEM(square, BF16), pltpu.VMEM(square, BF16),
            pltpu.VMEM(square, BF16), pltpu.VMEM(square, BF16), pltpu.VMEM(square, BF16),
            pltpu.VMEM(square, BF16),
            pltpu.VMEM(square, BF16), pltpu.VMEM(square, BF16), pltpu.VMEM(square, BF16),
            pltpu.VMEM(square, BF16), pltpu.VMEM(square, BF16),
            pltpu.VMEM((rows, 2 * order), BF16), pltpu.VMEM((columns, 2 * order), BF16),
            pltpu.VMEM((rows, columns), BF16),
            pltpu.SemaphoreType.DMA((col_count,)), pltpu.SemaphoreType.DMA((col_count,)),
            pltpu.SemaphoreType.DMA((3, 2 * col_count)), pltpu.SemaphoreType.DMA((2 * col_count,)),
            pltpu.SemaphoreType.DMA, pltpu.SemaphoreType.DMA((2,)),
        ],
        compiler_params=pltpu.CompilerParams(
            collective_id=0, has_side_effects=True, vmem_limit_bytes=60 * 2**20
        ),
        cost_estimate=pl.CostEstimate(flops=10**10, bytes_accessed=6 * 10**6, transcendentals=0),
    )(*rest)
    slow = pl.pallas_call(
        slow_kernel,
        out_shape=(
            jax.ShapeDtypeStruct(trailing.shape, BF16),
            jax.ShapeDtypeStruct(panels.shape, BF16),
        ),
        in_specs=[vmem, vmem, vmem, vmem, vmem, smem],
        out_specs=(vmem, vmem),
        scratch_shapes=[pltpu.VMEM(square, F32), pltpu.VMEM(square, F32)]
        + [pltpu.VMEM(square, BF16)] * 6
        + [pltpu.VMEM((rows, 2 * order), BF16), pltpu.VMEM((columns, 2 * order), BF16)],
        compiler_params=pltpu.CompilerParams(vmem_limit_bytes=48 * 2**20),
    )
    return lax.cond(
        residual[0, 0] < TOLERANCE,
        lambda *_: (updated, factor),
        lambda *args: tuple(slow(*args)),
        trailing, row_rows, col_rows, diagonals, coupling, sequence,
    )


def solution(mesh):
    return jax.shard_map(
        functools.partial(local, mesh.shape["col"], mesh.shape["row"]),
        mesh=mesh,
        in_specs=(P("row", "col"), P(None, ("row", "col"), None), P(), P(), P(), P(), P()),
        out_specs=(P("row", "col"), P(None, ("row", "col"), None)),
        check_vma=False,
    )
```
